32 devices in a mesh: groups: 2 (over y), seq: 4 (over x, core), head: 4 (over z).
Axes of the slice: x: 2, y: 2, z: 4, core: 2. Of those that a mesh axis runs over, the one named last changes fastest.
Arguments:
- lin_qkv: bfloat16 [8192, 3, 2048], P(('groups', 'seq'), None, 'head'), parts along dimension 0, may hold values from -6 to 6
- level_weights: float32 [16, 16], P(None, 'head'), may hold values from 0.3 to 1.7
- soft_q: bfloat16 [8192, 2048], P(('groups', 'seq'), 'head'), parts along dimension 0, may hold values from -6 to 6
- soft_kv: bfloat16 [8192, 2, 256], P(('groups', 'seq')), parts along dimension 0, may hold values from -6 to 6
Outputs:
- mixed: bfloat16 [8192, 2, 2048], P(('groups', 'seq'), None, 'head'), parts along dimension 0
The draws below stay inside these ranges and needn't reach their ends.
There are 2 independent parts, one for each index of `groups`. The reference program is written for one: setup_inputs(seed, part) draws one part's arguments, and reference() takes and returns one part's arrays. A program takes and returns all parts, laid end to end along the dimension named above; an argument that names none is the same for every part. Nothing has to cross between parts.
All inputs are finite; a program needn't handle non-finite values.
Results may differ from the reference program's by a relative error of at most 0.0049.
Values may be sent and summed in bfloat16 or wider, within the bound.
A program may use at most 128 MiB of HBM per device.

```python
import jax
import jax.numpy as jnp
from jax import lax

HD = 128
HEADS_LIN = 16
HEADS_SM = 16
KV_HEADS = 2
WINDOW = 1024
LEVELS = 16
TOK_DEV = 1024
TOKENS = 4096
N_SEQ = 4


def soft_inputs(key):
    query_key = jax.random.fold_in(key, 7001)
    pair_key = jax.random.fold_in(key, 7002)
    query_rows = jnp.clip(jax.random.normal(query_key, (TOKENS, HEADS_SM * HD), jnp.float32), -6.0, 6.0)
    pair_rows = jnp.clip(jax.random.normal(pair_key, (TOKENS, 2, KV_HEADS * HD), jnp.float32), -6.0, 6.0)
    return (query_rows, pair_rows)


def draw_soft_q(key, part):
    return soft_inputs(key)[0].astype(jnp.bfloat16)


def draw_soft_kv(key, part):
    return soft_inputs(key)[1].astype(jnp.bfloat16)


def shard_levels(rng, extent, cuts, low, top_value):
    loudness, own = 1.0, jax.random.fold_in(rng, 6)
    for axis_at, shards_of in cuts:
        heights = jnp.exp(jax.random.uniform(jax.random.fold_in(own, axis_at), (shards_of,), jnp.float32, low / len(cuts), top_value / len(cuts)))
        loudness = loudness * jnp.repeat(heights, extent[axis_at] // shards_of).reshape([-1 if axis == axis_at else 1 for axis in range(len(extent))])
    return loudness


def noise(own_key, extent, deviation, reach, cuts=(), held_as=jnp.bfloat16):
    gain = shard_levels(own_key, extent, cuts, -0.22, 0.18) if cuts else 1.0
    drawn = jax.random.normal(own_key, extent, jnp.float32) * deviation * gain
    return jnp.minimum(jnp.maximum(drawn, -reach), reach).astype(held_as)


def setup_inputs(seed: int = 0, part: int = 0) -> dict:
    key_of = jax.random.split(jax.random.key(seed), 5)
    part_keys = jax.random.split(jax.random.fold_in(key_of[4], part), 5)
    return {
        "lin_qkv": noise(part_keys[0], (TOKENS, 3, HEADS_LIN * HD), 1.0, 6.0, ((0, 4), (2, 4))),
        "level_weights": jnp.clip(0.3 + 1.40000004 * jax.random.uniform(key_of[1], (LEVELS, HEADS_LIN), jnp.float32) ** shard_levels(key_of[1], (LEVELS, HEADS_LIN), ((1, 4),), -0.2, 0.2), 0.3, 1.7),
        "soft_q": draw_soft_q(jax.random.fold_in(jax.random.fold_in(key_of[4], part), 71), part),
        "soft_kv": draw_soft_kv(jax.random.fold_in(jax.random.fold_in(key_of[4], part), 71), part),
    }


def bit_count(values):
    total = jnp.zeros_like(values)
    for power in range(LEVELS):
        total = total + (values >= 2 ** power).astype(jnp.int32)
    return total

def level_table(levels, table, first, count):
    result = jnp.zeros(levels.shape + (table.shape[1],), jnp.float32)
    for lev in range(first, first + count):
        result = result + (levels == lev).astype(jnp.float32)[..., None] * table[lev]
    return result

def reference(lin_qkv, level_weights, soft_q, soft_kv):
    heads = HEADS_LIN
    tok = TOK_DEV
    local_bits = tok.bit_length() - 1
    blocks_qkv = lin_qkv.reshape(N_SEQ, tok, 3, heads, HD)

    def local_part(block_qkv):
        query = block_qkv[:, 0].astype(jnp.float32)
        keys = block_qkv[:, 1].astype(jnp.float32)
        values = block_qkv[:, 2].astype(jnp.float32)
        pos = jnp.arange(tok, dtype=jnp.int32)
        levels = bit_count(jnp.bitwise_xor(pos[:, None], pos[None, :]))
        causal = pos[None, :] <= pos[:, None]
        weight = level_table(levels, level_weights, 0, local_bits + 1)
        weight = jnp.where(causal[:, :, None], weight, 0.0)
        scores = jnp.einsum('thd,shd->tsh', query, keys)
        weighted = (scores * weight).astype(jnp.bfloat16)
        intra = jnp.einsum('tsh,shd->thd', weighted.astype(jnp.float32), values)
        state = jnp.einsum('thd,the->hde', keys, values)
        return (intra, state)
    intra, states = lax.map(local_part, blocks_qkv)
    spans = jnp.arange(N_SEQ, dtype=jnp.int32)
    span_levels = local_bits + bit_count(jnp.bitwise_xor(spans[:, None], spans[None, :]))
    span_levels = jnp.where(spans[None, :] < spans[:, None], span_levels, 0)
    span_weight = level_table(span_levels, level_weights, 1, LEVELS - 1)
    span_weight = jnp.where((spans[None, :] < spans[:, None])[:, :, None], span_weight, 0.0)
    cross_state = jnp.einsum('cqh,qhde->chde', span_weight, states, precision=lax.Precision.HIGHEST).astype(jnp.bfloat16)
    query_all = blocks_qkv[:, :, 0].astype(jnp.float32)
    cross = jnp.einsum('cthd,chde->cthe', query_all, cross_state.astype(jnp.float32))
    lin_sum = intra + cross
    normed = lin_sum * lax.rsqrt(lax.optimization_barrier(jnp.mean(lin_sum * lin_sum, axis=-1, keepdims=True)) + 1e-06)
    lin_out = normed.astype(jnp.bfloat16).reshape(TOKENS, heads * HD)
    group = HEADS_SM // KV_HEADS
    block = min(512, TOK_DEV)
    queries = soft_q.reshape(TOKENS, HEADS_SM, HD)
    kv_all = soft_kv.reshape(TOKENS, 2, KV_HEADS, HD)
    padded = jnp.concatenate([jnp.zeros((WINDOW, 2, KV_HEADS, HD), jnp.bfloat16), kv_all], axis=0)
    scale = 1.0 / HD ** 0.5

    def one_block(index):
        start = (index * block).astype(jnp.int32)
        q_block = lax.dynamic_slice_in_dim(queries, start, block, 0).astype(jnp.float32)
        kv_block = lax.dynamic_slice_in_dim(padded, start, WINDOW + block, 0)
        keys = jnp.repeat(kv_block[:, 0], group, axis=1).astype(jnp.float32)
        values = jnp.repeat(kv_block[:, 1], group, axis=1).astype(jnp.float32)
        scores = jnp.einsum('ahd,jhd->haj', q_block, keys) * scale
        rows = jnp.arange(block, dtype=jnp.int32)[:, None]
        cols = jnp.arange(WINDOW + block, dtype=jnp.int32)[None, :]
        valid = (cols >= rows) & (cols <= rows + WINDOW) & (start + cols - WINDOW >= 0)
        scores = jnp.where(valid[None], scores, -1e+30)
        probs = jax.nn.softmax(scores, axis=-1).astype(jnp.bfloat16)
        out = jnp.einsum('haj,jhd->ahd', probs.astype(jnp.float32), values)
        return out.astype(jnp.bfloat16)
    soft_out = lax.map(one_block, jnp.arange(TOKENS // block, dtype=jnp.int32))
    soft_out = soft_out.reshape(TOKENS, HEADS_SM * HD)
    return jnp.stack([lin_out, soft_out], axis=1)
```

```python
import functools

import jax
import jax.numpy as jnp
from jax import lax
from jax.experimental import pallas as pl
from jax.experimental.pallas import tpu as pltpu
from jax.sharding import PartitionSpec as P

HD = 128
HEADS_SM = 16
KV_HEADS = 2
WINDOW = 1024
LEVELS = 16
MESH = pl.DeviceIdType.MESH
NEG = -1e30
LOG2E = 1.4426950408889634


def digits(value):
    total = 0
    for power in range(LEVELS):
        total = total + (value >= 2**power).astype(jnp.int32)
    return total


def kernel(
    n_seq,
    lin_ref,
    lw_ref,
    sq_ref,
    kv_ref,
    o_ref,
    kvx,
    wt,
    st,
    lin,
    inter,
    send,
    recv,
    kv_send_sem,
    kv_recv_sem,
    st_send_sem,
    st_recv_sem,
):
    tok = lin_ref.shape[1]
    heads = lin_ref.shape[2] // HD
    q_heads = sq_ref.shape[1] // HD
    chunk = wt.shape[1]
    half = chunk // 2
    chunks = tok // chunk
    half_bits = half.bit_length() - 1
    chunk_bits = chunk.bit_length() - 1
    local_bits = tok.bit_length() - 1
    me = lax.axis_index("seq")
    barrier = pltpu.get_barrier_semaphore()

    for k in range(1, n_seq):

        @pl.when(me >= k)
        def _():
            pl.semaphore_signal(barrier, inc=1, device_id={"seq": me - k}, device_id_type=MESH)

    def kv_copy(piece):
        rows = pl.ds(pl.multiple_of(piece * chunk, chunk), chunk)
        return pltpu.make_async_remote_copy(
            src_ref=kv_ref.at[:, rows, :],
            dst_ref=kvx.at[:, rows, :],
            send_sem=kv_send_sem.at[piece],
            recv_sem=kv_recv_sem.at[piece],
            device_id={"seq": me + 1},
            device_id_type=MESH,
        )

    def state_copy(k):
        return pltpu.make_async_remote_copy(
            src_ref=send,
            dst_ref=recv.at[k - 1],
            send_sem=st_send_sem.at[k - 1],
            recv_sem=st_recv_sem.at[k - 1],
            device_id={"seq": me + k},
            device_id_type=MESH,
        )

    def head_cols(h):
        return slice(h * HD, (h + 1) * HD)

    kvx[:, tok:, :] = kv_ref[...]

    @pl.when(me == 0)
    def _():
        kvx[:, :tok, :] = jnp.zeros((2, tok, HD), kvx.dtype)

    for h in range(heads):
        total = None
        for c in range(chunks):
            rows = slice(c * chunk, (c + 1) * chunk)
            state = lax.dot_general(
                lin_ref[1, rows, head_cols(h)],
                lin_ref[2, rows, head_cols(h)],
                (((0,), (0,)), ((), ())),
                preferred_element_type=jnp.float32,
            )
            st[h, c] = state
            total = state if total is None else total + state
        send[h] = total.astype(send.dtype)

    @pl.when(me < n_seq - 1)
    def _():
        pl.semaphore_wait(barrier, n_seq - 1 - me)
        for piece in range(chunks - 1, -1, -1):
            kv_copy(piece).start()

    for k in range(1, n_seq):

        @pl.when(me + k < n_seq)
        def _():
            state_copy(k).start()

    r = lax.broadcasted_iota(jnp.int32, (half, half), 0)
    s = lax.broadcasted_iota(jnp.int32, (half, half), 1)
    apart = jnp.bitwise_xor(r, s)
    for h in range(heads):
        table = jnp.full((half, half), lw_ref[0, h], jnp.float32)
        for lev in range(1, half_bits + 1):
            table = jnp.where(apart >= 2 ** (lev - 1), lw_ref[lev, h], table)
        table = jnp.where(s <= r, table, 0.0)
        wt[h, :half, :half] = table
        wt[h, half:, half:] = table
        wt[h, :half, half:] = jnp.zeros((half, half), jnp.float32)
        wt[h, half:, :half] = jnp.full((half, half), lw_ref[half_bits + 1, h], jnp.float32)

    @pl.loop(0, chunks)
    def _(c):
        rows = pl.ds(pl.multiple_of(c * chunk, chunk), chunk)
        for h in range(heads):
            scores = lax.dot_general(
                lin_ref[0, rows, head_cols(h)],
                lin_ref[1, rows, head_cols(h)],
                (((1,), (1,)), ((), ())),
                preferred_element_type=jnp.float32,
            )
            weighted = (scores * wt[h]).astype(jnp.bfloat16)
            lin[h, rows, :] = jnp.dot(
                weighted, lin_ref[2, rows, head_cols(h)], preferred_element_type=jnp.float32
            )

    r = lax.broadcasted_iota(jnp.int32, (chunk, chunk), 0)
    s = lax.broadcasted_iota(jnp.int32, (chunk, chunk), 1)
    ones = jnp.ones((chunk, HD), jnp.bfloat16)
    scale = LOG2E / HD**0.5

    @pl.loop(0, chunks)
    def _(step):
        block = chunks - 1 - step

        @pl.when(me > 0)
        def _():
            kv_copy(block).wait_recv()

        start = pl.multiple_of(block * chunk, chunk)
        for h in range(q_heads):
            query = sq_ref[pl.ds(start, chunk), head_cols(h)]
            scores = []
            for j in range(chunks + 1):
                keys = kvx[0, pl.ds(start + j * chunk, chunk), :]
                part = lax.dot_general(
                    query, keys, (((1,), (1,)), ((), ())), preferred_element_type=jnp.float32
                )
                if j < chunks:
                    here = (me > 0) | (block + j >= chunks)
                    part = part + jnp.where(here, 0.0, NEG)
                if j == 0:
                    part = jnp.where(s >= r, part, NEG)
                if j == chunks:
                    part = jnp.where(s <= r, part, NEG)
                scores.append(part)
            top = scores[0]
            for part in scores[1:]:
                top = jnp.maximum(top, part)
            top = jnp.max(top, axis=1, keepdims=True)
            out = jnp.zeros((chunk, 2 * HD), jnp.float32)
            for j in range(chunks + 1):
                values = kvx[1, pl.ds(start + j * chunk, chunk), :]
                probs = jnp.exp2((scores[j] - top) * scale).astype(jnp.bfloat16)
                out = out + jnp.dot(
                    probs,
                    jnp.concatenate([values, ones], axis=1),
                    preferred_element_type=jnp.float32,
                )
            inter[h, pl.ds(2 * start + 1, chunk, 2), :] = out[:, :HD] / out[:, HD:]

    for k in range(1, n_seq):

        @pl.when(me >= k)
        def _():
            state_copy(k).wait_recv()

    for h in range(heads):
        cross = jnp.zeros((HD, HD), jnp.float32)
        for k in range(1, n_seq):
            level = local_bits + digits(jnp.bitwise_xor(me, jnp.maximum(me - k, 0)))
            factor = lw_ref[level, h]
            cross = cross + jnp.where(me >= k, factor * recv[k - 1, h].astype(jnp.float32), 0.0)
        groups = [st[h, c] for c in range(chunks)]
        before = [cross] * chunks
        for bit in range(chunks.bit_length() - 1):
            factor = lw_ref[chunk_bits + bit + 1, h]
            for c in range(chunks):
                if (c >> bit) % 2:
                    before[c] = before[c] + factor * groups[(c >> bit) - 1]
            groups = [groups[2 * g] + groups[2 * g + 1] for g in range(len(groups) // 2)]
        for c in range(chunks):
            rows = slice(c * chunk, (c + 1) * chunk)
            total = lin[h, rows, :] + jnp.dot(
                lin_ref[0, rows, head_cols(h)],
                before[c].astype(jnp.bfloat16),
                preferred_element_type=jnp.float32,
            )
            mean = jnp.mean(total * total, axis=1, keepdims=True)
            inter[h, pl.ds(2 * c * chunk, chunk, 2), :] = total * lax.rsqrt(mean + 1e-06)
            both = slice(2 * c * chunk, 2 * (c + 1) * chunk)
            o_ref[both, head_cols(h)] = inter[h, both, :].astype(o_ref.dtype)

    @pl.when(me < n_seq - 1)
    def _():
        for piece in range(chunks):
            kv_copy(piece).wait_send()

    for k in range(1, n_seq):

        @pl.when(me + k < n_seq)
        def _():
            state_copy(k).wait_send()


def local(lin_qkv, level_weights, soft_q, soft_kv):
    tok = lin_qkv.shape[0]
    heads = lin_qkv.shape[2] // HD
    q_heads = soft_q.shape[1] // HD
    assert tok == WINDOW and heads == q_heads
    n_seq = lax.axis_size("seq")
    chunk = min(256, tok)
    chunks = tok // chunk
    kv_index = lax.axis_index("head") * q_heads // (HEADS_SM // KV_HEADS)
    own_kv = lax.dynamic_slice_in_dim(soft_kv, kv_index * HD, HD, 2)
    vmem = pl.BlockSpec(memory_space=pltpu.VMEM)
    out = pl.pallas_call(
        functools.partial(kernel, n_seq),
        out_shape=jax.ShapeDtypeStruct((2 * tok, heads * HD), jnp.bfloat16),
        in_specs=[vmem, pl.BlockSpec(memory_space=pltpu.SMEM), vmem, vmem],
        out_specs=vmem,
        scratch_shapes=[
            pltpu.VMEM((2, 2 * tok, HD), jnp.bfloat16),
            pltpu.VMEM((heads, chunk, chunk), jnp.float32),
            pltpu.VMEM((heads, chunks, HD, HD), jnp.float32),
            pltpu.VMEM((heads, tok, HD), jnp.float32),
            pltpu.VMEM((heads, 2 * tok, HD), jnp.float32),
            pltpu.VMEM((heads, HD, HD), jnp.bfloat16),
            pltpu.VMEM((n_seq - 1, heads, HD, HD), jnp.bfloat16),
            pltpu.SemaphoreType.DMA((chunks,)),
            pltpu.SemaphoreType.DMA((chunks,)),
            pltpu.SemaphoreType.DMA((n_seq - 1,)),
            pltpu.SemaphoreType.DMA((n_seq - 1,)),
        ],
        compiler_params=pltpu.CompilerParams(
            collective_id=0, has_side_effects=True, vmem_limit_bytes=48 * 1024 * 1024
        ),
    )(jnp.transpose(lin_qkv, (1, 0, 2)), level_weights, soft_q, jnp.transpose(own_kv, (1, 0, 2)))
    return out.reshape(tok, 2, heads * HD)


def solution(mesh):
    in_specs = (
        P(("groups", "seq"), None, "head"),
        P(None, "head"),
        P(("groups", "seq"), "head"),
        P(("groups", "seq"), None, None),
    )
    out_specs = P(("groups", "seq"), None, "head")
    return jax.shard_map(local, mesh=mesh, in_specs=in_specs, out_specs=out_specs, check_vma=False)
```

```python
import functools

import jax
import jax.numpy as jnp
from jax import lax
from jax.experimental import pallas as pl
from jax.experimental.pallas import tpu as pltpu
from jax.sharding import PartitionSpec as P

HD = 128
HEADS_SM = 16
KV_HEADS = 2
WINDOW = 1024
MESH = pl.DeviceIdType.MESH
NEG = -1e30
LOG2E = 1.4426950408889634


def kernel(
    n_seq,
    paired,
    lin_hbm,
    lw_ref,
    sq_hbm,
    kv_ref,
    o_ref,
    lin_ref,
    sq_ref,
    in_sem,
    kvx,
    wt,
    st,
    lin,
    inter,
    gsum,
    cross,
    send,
    recv,
    kv_send_sem,
    kv_recv_sem,
    hop_send_sem,
    hop_recv_sem,
    st_send_sem,
    st_recv_sem,
):
    tok = lin_ref.shape[1]
    heads = lin_ref.shape[2] // HD
    q_heads = sq_ref.shape[1] // HD
    chunk = wt.shape[1]
    half = chunk // 2
    chunks = tok // chunk
    half_bits = half.bit_length() - 1
    chunk_bits = chunk.bit_length() - 1
    local_bits = tok.bit_length() - 1
    me = lax.axis_index("seq")
    barrier = pltpu.get_barrier_semaphore()
    loads = [
        pltpu.make_async_copy(lin_hbm.at[1:3], lin_ref.at[1:3], in_sem.at[0]),
        pltpu.make_async_copy(lin_hbm.at[0], lin_ref.at[0], in_sem.at[1]),
        pltpu.make_async_copy(sq_hbm, sq_ref, in_sem.at[2]),
    ]
    for load in loads:
        load.start()

    stages = n_seq.bit_length() - 1
    side = me % 2
    my_head = lax.axis_index("head")
    part_of = my_head % 2
    relayed = (me % 2 == 0) & (me > 0) & paired
    relays = (me % 2 == 1) & (me < n_seq - 1) & paired

    def partner_at(bit):
        upper = (me // 2**bit) % 2
        return me + 2**bit - 2 ** (bit + 1) * upper

    @pl.when(me > 0)
    def _():
        pl.semaphore_signal(barrier, inc=1, device_id={"seq": me - 1}, device_id_type=MESH)

    for bit in range(stages):
        pl.semaphore_signal(
            barrier, inc=1, device_id={"seq": partner_at(bit)}, device_id_type=MESH
        )
    if paired:
        other_head = my_head + 1 - 2 * part_of
        pl.semaphore_signal(barrier, inc=1, device_id={"head": other_head}, device_id_type=MESH)

    def piece_rows(piece):
        return slice(piece * chunk, (piece + 1) * chunk)

    def kv_copy(piece, which):
        return pltpu.make_async_remote_copy(
            src_ref=kv_ref.at[which, piece_rows(piece), :],
            dst_ref=kvx.at[which, piece_rows(piece), :],
            send_sem=kv_send_sem.at[piece, which],
            recv_sem=kv_recv_sem.at[piece, which],
            device_id={"seq": me + 1},
            device_id_type=MESH,
        )

    def hop_copy(piece, which):
        return pltpu.make_async_remote_copy(
            src_ref=kvx.at[which, piece_rows(piece), :],
            dst_ref=kvx.at[which, piece_rows(piece), :],
            send_sem=hop_send_sem.at[piece],
            recv_sem=hop_recv_sem.at[piece],
            device_id={"head": other_head},
            device_id_type=MESH,
        )

    def state_copy(bit, near):
        if bit == 0:
            src, dst, target = send.at[0], recv.at[0], partner_at(0)
        else:
            rows = pl.ds(pl.multiple_of(side * (HD // 2), HD // 2), HD // 2)
            src = recv.at[bit, :, rows, :] if near else send.at[bit, :, rows, :]
            dst = recv.at[bit, :, rows, :]
            target = partner_at(0) if near else partner_at(bit)
        return pltpu.make_async_remote_copy(
            src_ref=src,
            dst_ref=dst,
            send_sem=st_send_sem.at[bit, int(near)],
            recv_sem=st_recv_sem.at[bit, int(near)],
            device_id={"seq": target},
            device_id_type=MESH,
        )

    def near_arrival(bit):
        rows = pl.ds(pl.multiple_of((1 - side) * (HD // 2), HD // 2), HD // 2)
        return pltpu.make_async_remote_copy(
            src_ref=recv.at[bit, :, rows, :],
            dst_ref=recv.at[bit, :, rows, :],
            send_sem=st_send_sem.at[bit, 1],
            recv_sem=st_recv_sem.at[bit, 1],
            device_id={"seq": partner_at(0)},
            device_id_type=MESH,
        )

    def guarded(bit, upper, call):
        if bit == 0 or bit + 1 < stages:
            call()
        else:
            pl.when((me // 2**bit) % 2 == int(upper))(call)

    def send_far(bit):
        guarded(bit, False, lambda: state_copy(bit, False).start())

    def take_stage(bit):
        upper = (me // 2**bit) % 2 == 1
        for h in range(heads):
            got = recv[bit, h].astype(jnp.float32)
            factor = jnp.where(upper, lw_ref[h, local_bits + bit + 1], 0.0)
            added = factor * got
            cross[h] = added if bit == 0 else cross[h] + added
            if bit + 1 < stages:
                total = gsum[h] + got
                gsum[h] = total
                send[bit + 1, h] = total.astype(send.dtype)

    def head_cols(h):
        return slice(h * HD, (h + 1) * HD)

    kvx[:, tok:, :] = kv_ref[...]

    @pl.when(me == 0)
    def _():
        kvx[0, :tok, :] = jnp.broadcast_to(kv_ref[0, 0:1, :], (tok, HD))
        kvx[1, :tok, :] = jnp.zeros((tok, HD), kvx.dtype)

    r = lax.broadcasted_iota(jnp.int32, (half, half), 0)
    s = lax.broadcasted_iota(jnp.int32, (half, half), 1)
    apart = jnp.bitwise_xor(r, s)
    for h in range(heads):
        table = jnp.full((half, half), lw_ref[h, 0], jnp.float32)
        for lev in range(1, half_bits + 1):
            table = jnp.where(apart >= 2 ** (lev - 1), lw_ref[h, lev], table)
        table = jnp.where(s <= r, table, 0.0)
        wt[h, :half, :half] = table
        wt[h, half:, half:] = table
        wt[h, :half, half:] = jnp.zeros((half, half), jnp.float32)
        wt[h, half:, :half] = jnp.full((half, half), lw_ref[h, half_bits + 1], jnp.float32)

    pl.semaphore_wait(barrier, stages + int(paired) + (me < n_seq - 1).astype(jnp.int32))

    @pl.when((me < n_seq - 1) & jnp.logical_not(relays))
    def _():
        for piece in range(chunks - 1, -1, -1):
            for which in range(2):
                kv_copy(piece, which).start()

    @pl.when(relays)
    def _():
        for piece in range(chunks - 1, -1, -1):
            kv_copy(piece, part_of).start()

    loads[0].wait()
    for h in range(heads):
        total = None
        for c in range(chunks):
            rows = slice(c * chunk, (c + 1) * chunk)
            state = lax.dot_general(
                lin_ref[1, rows, head_cols(h)],
                lin_ref[2, rows, head_cols(h)],
                (((0,), (0,)), ((), ())),
                preferred_element_type=jnp.float32,
            )
            st[h, c] = state
            total = state if total is None else total + state
        gsum[h] = total
        send[0, h] = total.astype(send.dtype)

    state_copy(0, False).start()

    loads[1].wait()
    for c in range(chunks):
        rows = slice(c * chunk, (c + 1) * chunk)
        for h in range(heads):
            scores = lax.dot_general(
                lin_ref[0, rows, head_cols(h)],
                lin_ref[1, rows, head_cols(h)],
                (((1,), (1,)), ((), ())),
                preferred_element_type=jnp.float32,
            )
            weighted = (scores * wt[h]).astype(jnp.bfloat16)
            lin[h, rows, :] = jnp.dot(
                weighted, lin_ref[2, rows, head_cols(h)], preferred_element_type=jnp.float32
            )
        if paired:
            piece = chunks - 1 - c

            @pl.when(relayed)
            def _():
                kv_copy(piece, part_of).wait_recv()
                hop_copy(piece, part_of).start()

    state_copy(0, False).wait_recv()
    take_stage(0)
    if stages > 1:
        send_far(1)
    loads[2].wait()

    group = 2
    r = lax.broadcasted_iota(jnp.int32, (chunk, chunk), 0)
    s = lax.broadcasted_iota(jnp.int32, (chunk, chunk), 1)
    ones = jnp.ones((chunk, HD), jnp.bfloat16)
    ones_before = jnp.where(me > 0, ones, 0)
    scale = LOG2E / HD**0.5
    units = [(b, g) for b in range(chunks - 1, -1, -1) for g in range(q_heads // group)]

    def part_scores(unit, j):
        block, g = unit
        queries = jnp.concatenate(
            [
                sq_ref[block * chunk : (block + 1) * chunk, head_cols(g * group + i)]
                for i in range(group)
            ],
            axis=0,
        )
        part = lax.dot_general(
            queries,
            kvx[0, (block + j) * chunk : (block + j + 1) * chunk, :],
            (((1,), (1,)), ((), ())),
            preferred_element_type=jnp.float32,
        ).reshape(group, chunk, chunk)
        if j == 0:
            part = jnp.where((s >= r)[None], part, NEG)
        if j == chunks:
            part = jnp.where((s <= r)[None], part, NEG)
        return part

    def wait_piece(unit):
        block, g = unit
        if g == 0:

            @pl.when((me > 0) & jnp.logical_not(relayed))
            def _():
                kv_copy(block, 0).wait_recv()
                kv_copy(block, 1).wait_recv()

            if paired:

                @pl.when(relayed)
                def _():
                    hop_copy(block, 1 - part_of).wait_recv()

    def far_arrived(bit):
        state_copy(bit, False).wait_recv()
        state_copy(bit, True).start()

    def near_arrived(bit):
        near_arrival(bit).wait_recv()
        take_stage(bit)
        if bit + 1 < stages:
            send_far(bit + 1)

    per_block = q_heads // group
    later = []
    for bit in range(1, stages):
        at = min((2 * bit - 1) * per_block - 1, len(units) - 1)
        later.append((at, functools.partial(far_arrived, bit)))
        at = min(2 * bit * per_block - 1, len(units) - 1)
        later.append((at, functools.partial(near_arrived, bit)))

    wait_piece(units[0])
    scores = [part_scores(units[0], j) for j in range(chunks + 1)]
    for index, unit in enumerate(units):
        block, g = unit
        top = scores[0]
        for part in scores[1:]:
            top = jnp.maximum(top, part)
        top = jnp.max(top, axis=2, keepdims=True)
        following = []
        if index + 1 < len(units):
            wait_piece(units[index + 1])
        out = jnp.zeros((group * chunk, 2 * HD), jnp.float32)
        for j in range(chunks + 1):
            if index + 1 < len(units):
                following.append(part_scores(units[index + 1], j))
            values = kvx[1, (block + j) * chunk : (block + j + 1) * chunk, :]
            counts = ones_before if block + j < chunks else ones
            probs = jnp.exp2((scores[j] - top) * scale).astype(jnp.bfloat16)
            out = out + jnp.dot(
                probs.reshape(group * chunk, chunk),
                jnp.concatenate([values, counts], axis=1),
                preferred_element_type=jnp.float32,
            )
        mean = out[:, :HD] / out[:, HD:]
        for i in range(group):
            inter[g * group + i, pl.ds(2 * block * chunk + 1, chunk, 2), :] = mean[
                i * chunk : (i + 1) * chunk
            ]
        scores = following
        for at, call in later:
            if at == index:
                guarded(call.args[0], True, call)

    for h in range(heads):
        groups = [st[h, c] for c in range(chunks)]
        before = [cross[h]] * chunks
        for bit in range(chunks.bit_length() - 1):
            factor = lw_ref[h, chunk_bits + bit + 1]
            for c in range(chunks):
                if (c >> bit) % 2:
                    before[c] = before[c] + factor * groups[(c >> bit) - 1]
            groups = [groups[2 * g] + groups[2 * g + 1] for g in range(len(groups) // 2)]
        for c in range(chunks):
            rows = slice(c * chunk, (c + 1) * chunk)
            total = lin[h, rows, :] + jnp.dot(
                lin_ref[0, rows, head_cols(h)],
                before[c].astype(jnp.bfloat16),
                preferred_element_type=jnp.float32,
            )
            mean = jnp.mean(total * total, axis=1, keepdims=True)
            inter[h, pl.ds(2 * c * chunk, chunk, 2), :] = total * lax.rsqrt(mean + 1e-06)
            both = slice(2 * c * chunk, 2 * (c + 1) * chunk)
            o_ref[both, head_cols(h)] = inter[h, both, :].astype(o_ref.dtype)

    @pl.when((me < n_seq - 1) & jnp.logical_not(relays))
    def _():
        for piece in range(chunks):
            for which in range(2):
                kv_copy(piece, which).wait_send()

    if paired:

        @pl.when(relays)
        def _():
            for piece in range(chunks):
                kv_copy(piece, part_of).wait_send()

        @pl.when(relayed)
        def _():
            for piece in range(chunks):
                hop_copy(piece, part_of).wait_send()

    state_copy(0, False).wait_send()
    for bit in range(1, stages):
        guarded(bit, False, functools.partial(lambda b: state_copy(b, False).wait_send(), bit))
        guarded(bit, True, functools.partial(lambda b: state_copy(b, True).wait_send(), bit))


def local(lin_qkv, level_weights, soft_q, soft_kv):
    tok = lin_qkv.shape[0]
    heads = lin_qkv.shape[2] // HD
    q_heads = soft_q.shape[1] // HD
    assert tok == WINDOW and heads == q_heads
    n_seq = lax.axis_size("seq")
    stages = n_seq.bit_length() - 1
    paired = HEADS_SM // KV_HEADS % (2 * q_heads) == 0 and lax.axis_size("head") % 2 == 0
    chunk = min(256, tok)
    chunks = tok // chunk
    kv_index = lax.axis_index("head") * q_heads // (HEADS_SM // KV_HEADS)
    own_kv = lax.dynamic_slice_in_dim(soft_kv, kv_index * HD, HD, 2)
    vmem = pl.BlockSpec(memory_space=pltpu.VMEM)
    hbm = pl.BlockSpec(memory_space=pltpu.MemorySpace.HBM)
    out = pl.pallas_call(
        functools.partial(kernel, n_seq, paired),
        out_shape=jax.ShapeDtypeStruct((2 * tok, heads * HD), jnp.bfloat16),
        in_specs=[hbm, pl.BlockSpec(memory_space=pltpu.SMEM), hbm, vmem],
        out_specs=vmem,
        scratch_shapes=[
            pltpu.VMEM((3, tok, heads * HD), jnp.bfloat16),
            pltpu.VMEM((tok, q_heads * HD), jnp.bfloat16),
            pltpu.SemaphoreType.DMA((3,)),
            pltpu.VMEM((2, 2 * tok, HD), jnp.bfloat16),
            pltpu.VMEM((heads, chunk, chunk), jnp.float32),
            pltpu.VMEM((heads, chunks, HD, HD), jnp.float32),
            pltpu.VMEM((heads, tok, HD), jnp.float32),
            pltpu.VMEM((heads, 2 * tok, HD), jnp.float32),
            pltpu.VMEM((heads, HD, HD), jnp.float32),
            pltpu.VMEM((heads, HD, HD), jnp.float32),
            pltpu.VMEM((stages, heads, HD, HD), jnp.bfloat16),
            pltpu.VMEM((stages, heads, HD, HD), jnp.bfloat16),
            pltpu.SemaphoreType.DMA((chunks, 2)),
            pltpu.SemaphoreType.DMA((chunks, 2)),
            pltpu.SemaphoreType.DMA((chunks,)),
            pltpu.SemaphoreType.DMA((chunks,)),
            pltpu.SemaphoreType.DMA((stages, 2)),
            pltpu.SemaphoreType.DMA((stages, 2)),
        ],
        compiler_params=pltpu.CompilerParams(
            collective_id=0, has_side_effects=True, vmem_limit_bytes=48 * 1024 * 1024
        ),
    )(jnp.transpose(lin_qkv, (1, 0, 2)), level_weights.T, soft_q, jnp.transpose(own_kv, (1, 0, 2)))
    return out.reshape(tok, 2, heads * HD)


def solution(mesh):
    in_specs = (
        P(("groups", "seq"), None, "head"),
        P(None, "head"),
        P(("groups", "seq"), "head"),
        P(("groups", "seq"), None, None),
    )
    out_specs = P(("groups", "seq"), None, "head")
    return jax.shard_map(local, mesh=mesh, in_specs=in_specs, out_specs=out_specs, check_vma=False)
```
